32 devices in a mesh: groups: 2 (over y), dp: 4 (over z), tensor: 2 (over x), section: 2 (over core).
Axes of the slice: x: 2, y: 2, z: 4, core: 2. Of those that a mesh axis runs over, the one named last changes fastest.
Arguments:
- tokens: bfloat16 [512, 8192], P(('groups', 'dp'), 'tensor'), parts along dimension 0, may hold values from -120 to 120
- norm_gain: float32 [8192], P('tensor'), may hold values from 0.25 to 1.75
- gate_weight: bfloat16 [8192, 24576], P('tensor', ('dp', 'section')), may hold values from -0.0625 to 0.0625
- up_weight: bfloat16 [8192, 24576], P('tensor', ('dp', 'section')), may hold values from -0.0625 to 0.0625
- down_weight: bfloat16 [24576, 8192], P(('dp', 'section'), 'tensor'), may hold values from -0.0390625 to 0.0390625
- lengths: int32 [8], P('groups'), parts along dimension 0, may hold values from 1 to 64, 96 in all
Outputs:
- mixed: bfloat16 [512, 8192], P(('groups', 'dp', 'section'), 'tensor'), parts along dimension 0
The draws below stay inside these ranges and needn't reach their ends.
There are 2 independent parts, one for each index of `groups`. The reference program is written for one: setup_inputs(seed, part) draws one part's arguments, and reference() takes and returns one part's arrays. A program takes and returns all parts, laid end to end along the dimension named above; an argument that names none is the same for every part. Nothing has to cross between parts.
Inputs may be any that keep to these rules, and one draw needn't show every extreme that they name: lengths[i] live rows stand at the head of data shard i's 64 slots; the lengths sum to 96 and the largest equals 64.
All inputs are finite; a program needn't handle non-finite values.
Results may differ from the reference program's by a relative error of at most 0.019.
Values may be sent and summed in bfloat16 or wider, within the bound.
A program may use at most 192 MiB of HBM per device.

```python
import math
import jax
import jax.numpy as jnp
import numpy as np
from jax import lax

D = 8192
FF = 24576
CAP = 64
TOKENS = 256
LIVE = 96
N_DP = 4
N_TENSOR = 2
N_SECTION = 2


def draw_tokens(key, part):
    key = jax.random.fold_in(key, 11)
    noise_key, row_key, column_key = jax.random.split(key, 3)
    column = jnp.arange(D, dtype=jnp.float32) / D
    spread = jnp.exp(jax.random.uniform(column_key, (1, D), jnp.float32, math.log(0.5), math.log(5.0)))
    noise = jnp.clip(jax.random.normal(noise_key, (TOKENS, D), jnp.float32), -6.0, 6.0)
    column_trend = jnp.sqrt(0.5 + column)
    row_scale = jnp.exp(jax.random.uniform(row_key, (TOKENS, 1), jnp.float32, math.log(0.3), math.log(3.0)))
    return (noise * column_trend[None, :] * spread * row_scale).astype(jnp.bfloat16)


def block_levels(rng, dims, cuts, least, high):
    def one(axis_at, parts):
        heights = jax.random.uniform(jax.random.fold_in(jax.random.fold_in(rng, 6), axis_at), (parts,), jnp.float32, least / len(cuts), high / len(cuts))
        return jnp.repeat(jnp.exp(heights), dims[axis_at] // parts).reshape((-1,) + (1,) * (len(dims) - axis_at - 1))

    loudness = one(*cuts[0])
    for cut in cuts[1:]:
        loudness = loudness * one(*cut)
    return loudness


def length_profile(number_of, total, reach, slope):
    portions = [(1 << 20) // math.isqrt(standing ** slope) + 1 for standing in range(2, number_of + 1)]
    rest, counts = total - reach - (number_of - 1), [1] * (number_of - 1)
    while rest > 0:
        candidates = [i for i in range(number_of - 1) if counts[i] < reach]
        whole, left = sum([portions[i] for i in candidates]), rest
        for i in candidates:
            addition = min(reach - counts[i], max(1, left * portions[i] // whole), rest)
            counts[i] = counts[i] + addition
            rest = rest - addition
    return np.array([reach] + counts)


def ragged_sizes(rng, count, total, reach, lean):
    if count == 2:
        one = jax.random.randint(rng, (), max(1, total - reach), min(reach, total - 1) + 1)
        return jnp.stack([one, total - one])
    sizes = jnp.asarray(length_profile(count, total, reach, lean), jnp.int32)
    twos = (count - 1) // 2
    source_of, taker = sizes[1:1 + 2 * twos:2], sizes[2:2 + 2 * twos:2]
    slack = jnp.minimum(source_of - 1, reach - taker)
    moved = jax.random.randint(jax.random.fold_in(rng, 1), (twos,), 0, 1 << 20) % (slack + 1)
    sizes = sizes.at[1:1 + 2 * twos:2].set(source_of - moved).at[2:2 + 2 * twos:2].set(taker + moved)
    return sizes[jax.random.permutation(jax.random.fold_in(rng, 2), count)]


def scatter_about(key, extent, width, reach, pieces=(), kind=jnp.bfloat16):
    entries = width * jax.random.normal(key, extent, jnp.float32)
    if pieces:
        entries = entries * block_levels(key, extent, pieces, -0.22, 0.18)
    return jnp.clip(entries, -reach, reach).astype(kind)


def setup_inputs(seed: int = 0, part: int = 0) -> dict:
    seeds = jax.random.split(jax.random.key(seed), 7)
    own_keys = jax.random.split(jax.random.fold_in(seeds[6], part), 7)
    return {
        "tokens": draw_tokens(jax.random.fold_in(jax.random.fold_in(seeds[6], part), 71), part),
        "norm_gain": jnp.clip(1.0 + 0.15 * jax.random.normal(seeds[1], (D,), jnp.float32), 0.25, 1.75),
        "gate_weight": scatter_about(seeds[2], (D, FF), D ** -0.5, 0.0625, ((0, 2), (1, 8))),
        "up_weight": scatter_about(seeds[3], (D, FF), D ** -0.5, 0.0625, ((0, 2), (1, 8))),
        "down_weight": scatter_about(seeds[4], (FF, D), FF ** -0.5, 0.0390625, ((0, 8), (1, 2))),
        "lengths": ragged_sizes(own_keys[5], N_DP, LIVE, CAP, 2).astype(jnp.int32),
    }


norm_epsilon = 1e-05

def rounded(values):
    return lax.optimization_barrier(values.astype(jnp.bfloat16)).astype(jnp.float32)

def reference(tokens, norm_gain, gate_weight, up_weight, down_weight, lengths):
    widened = tokens.astype(jnp.float32)
    squares = lax.optimization_barrier(jnp.sum(widened * widened, axis=1))
    scaling = lax.rsqrt(squares / D + norm_epsilon)
    normed = (widened * scaling[:, None] * norm_gain[None, :]).astype(jnp.bfloat16)
    both_weights = jnp.concatenate([gate_weight, up_weight], axis=1)
    block_width = D // N_TENSOR
    summed = jnp.zeros((TOKENS, 2 * FF), jnp.float32)
    for block_index in range(N_TENSOR):
        lower = block_index * block_width
        block_term = jnp.dot(normed[:, lower:lower + block_width], both_weights[lower:lower + block_width], preferred_element_type=jnp.float32)
        summed = summed + rounded(block_term)
    hidden = (jax.nn.silu(summed[:, :FF]) * summed[:, FF:]).astype(jnp.bfloat16)
    groups = N_DP * N_SECTION
    unit_span = FF // groups
    branch = jnp.zeros((TOKENS, D), jnp.float32)
    for block_index in range(groups):
        lower = block_index * unit_span
        block_term = jnp.dot(hidden[:, lower:lower + unit_span], down_weight[lower:lower + unit_span], preferred_element_type=jnp.float32)
        branch = branch + rounded(block_term)
    row_number = jnp.arange(TOKENS, dtype=jnp.int32)
    slot_of = row_number % CAP
    shard_of = row_number // CAP
    live_row = slot_of < lengths[shard_of]
    return jnp.where(live_row[:, None], branch, 0.0).astype(jnp.bfloat16)
```

```python
import functools

import jax
import jax.numpy as jnp
from jax import lax
from jax.experimental import pallas as pl
from jax.experimental.pallas import tpu as pltpu
from jax.sharding import PartitionSpec as P

norm_epsilon = 1e-05
f32, bf16 = jnp.float32, jnp.bfloat16
MESH = pl.DeviceIdType.MESH
LAG = 3


def aligned(value, unit):
    return pl.multiple_of(value, unit)


def kernel(
    size,
    tokens, gain, gate_weight, up_weight, down_weight, lengths, out,
    tok, gate_buf, up_buf, down_buf,
    own, right_out, right_in, left_out, left_in, rows, normed, squares, squares_in,
    part, part_in, hidden,
    partial, sib_out, sib_in, zright_out, zright_in, zleft_out, zleft_in, final_out, out_buf,
    tok_sem, gate_sem, up_sem, down_sem,
    ring_send, ring_recv, rows_send, rows_recv, squares_send, squares_recv,
    part_send, part_recv, hidden_send, hidden_recv,
    sib_send, sib_recv, zring_send, zring_recv, final_send, final_recv, out_sem,
):
    n, nt, live, slots = size["n"], size["nt"], size["live"], size["slots"]
    ka, wa, nc, wu, nb, nj, wj = (size[x] for x in ("ka", "wa", "nc", "wu", "nb", "nj", "wj"))
    width = tokens.shape[1]
    half, hj, hs, rt = width // 2, wj // 2, slots // 2, live // nt
    z, t, s = lax.axis_index("dp"), lax.axis_index("tensor"), lax.axis_index("section")
    peers = [lax.rem(t + i, nt) for i in range(1, nt)]
    sib = {"section": 1 - s}
    far = jnp.maximum(z, n - 1 - z)

    def gate_copy(c):
        slot = lax.rem(c, nb)
        cols = pl.ds(aligned(c * wu, 128), wu)
        return (
            pltpu.make_async_copy(gate_weight.at[:, cols], gate_buf.at[slot], gate_sem.at[slot]),
            pltpu.make_async_copy(up_weight.at[:, cols], up_buf.at[slot], up_sem.at[slot]),
        )

    def down_copy(j):
        return pltpu.make_async_copy(
            down_weight.at[:, pl.ds(aligned(j * wj, 128), wj)], down_buf.at[j], down_sem.at[j]
        )

    def remote(src, dst, send, recv, where):
        return pltpu.make_async_remote_copy(
            src_ref=src, dst_ref=dst, send_sem=send, recv_sem=recv, device_id=where,
            device_id_type=MESH,
        )

    tok_copy = pltpu.make_async_copy(tokens, tok, tok_sem)
    tok_copy.start()

    @pl.loop(0, nb)
    def _(c):
        for copy in gate_copy(c):
            copy.start()

    @pl.loop(0, nj)
    def _(j):
        down_copy(j).start()

    barrier = pltpu.get_barrier_semaphore()
    for p in peers:
        pl.semaphore_signal(barrier, inc=1, device_id={"tensor": p}, device_id_type=MESH)
    pl.semaphore_signal(barrier, inc=1, device_id=sib, device_id_type=MESH)

    @pl.when(z > 0)
    def _():
        pl.semaphore_signal(barrier, inc=1, device_id={"dp": z - 1}, device_id_type=MESH)

    @pl.when(z < n - 1)
    def _():
        pl.semaphore_signal(barrier, inc=1, device_id={"dp": z + 1}, device_id_type=MESH)

    start = jnp.int32(0)
    mine = jnp.int32(0)
    for i in range(n):
        start = start + jnp.where(i < z, lengths[i], 0)
        mine = mine + jnp.where(i == z, lengths[i], 0)

    place_row = lax.broadcasted_iota(jnp.int32, (live, slots), 0)
    place_slot = lax.broadcasted_iota(jnp.int32, (live, slots), 1)
    place = jnp.where(
        (place_row == place_slot + start) & (place_slot < mine), 1.0, 0.0
    ).astype(bf16)

    @pl.when(z == 0)
    def _():
        right_in[...] = jnp.zeros_like(right_in)
        zright_in[...] = jnp.zeros_like(zright_in)

    @pl.when(z == n - 1)
    def _():
        left_in[...] = jnp.zeros_like(left_in)
        zleft_in[...] = jnp.zeros_like(zleft_in)

    tok_copy.wait()
    for k in range(ka):
        cols = pl.ds(aligned(s * half + k * wa, 128), wa)
        own[k] = jnp.dot(place, tok[:, cols], preferred_element_type=f32).astype(bf16)

    pl.semaphore_wait(
        barrier, nt + jnp.where(z > 0, 1, 0) + jnp.where(z < n - 1, 1, 0)
    )

    def right_copy(k):
        return remote(right_out.at[k], right_in.at[k], ring_send.at[0, k], ring_recv.at[0, k],
                      {"dp": jnp.where(z < n - 1, z + 1, z - 1)})

    def left_copy(k):
        return remote(left_out.at[k], left_in.at[k], ring_send.at[1, k], ring_recv.at[1, k],
                      {"dp": jnp.where(z > 0, z - 1, z + 1)})

    def rows_copy(k, side):
        cols = pl.ds(aligned(side * half + k * wa, 128), wa)
        return remote(rows.at[:, cols], rows.at[:, cols], rows_send.at[k], rows_recv.at[k], sib)

    squares[...] = jnp.zeros_like(squares)

    def absorb(k, side):
        cols = pl.ds(aligned(side * half + k * wa, 128), wa)
        wide = rows[:, cols].astype(f32)
        total = squares[...]
        for q in range(wa // 128):
            piece = wide[:, q * 128:(q + 1) * 128]
            total = total + piece * piece
        squares[...] = total
        normed[:, cols] = (wide * gain[:, cols]).astype(bf16)

    @pl.loop(0, ka + n - 1)
    def _(m):
        kr, kl, kx = m - z, m - (n - 1 - z), m - far

        @pl.when((kr >= 0) & (kr < ka))
        def _():
            @pl.when(z > 0)
            def _():
                right_copy(kr).wait_recv()

            @pl.when(z < n - 1)
            def _():
                right_out[kr] = own[kr] + right_in[kr]
                right_copy(kr).start()

        @pl.when((kl >= 0) & (kl < ka))
        def _():
            @pl.when(z < n - 1)
            def _():
                left_copy(kl).wait_recv()

            @pl.when(z > 0)
            def _():
                left_out[kl] = own[kl] + left_in[kl]
                left_copy(kl).start()

        @pl.when((kx >= 0) & (kx < ka))
        def _():
            cols = pl.ds(aligned(s * half + kx * wa, 128), wa)
            rows[:, cols] = own[kx] + right_in[kx] + left_in[kx]
            rows_copy(kx, s).start()
            absorb(kx, s)

    @pl.loop(0, ka)
    def _(k):
        rows_copy(k, 1 - s).wait_recv()
        absorb(k, 1 - s)

    my_rows = pl.ds(aligned(t * rt, 16), rt)

    def rows_of(p):
        return pl.ds(aligned(p * rt, 16), rt)

    def squares_copy(p):
        return remote(squares.at[rows_of(p)], squares_in.at[t], squares_send.at[p],
                      squares_recv.at[t], {"tensor": p})

    def squares_arrival(p):
        return remote(squares.at[rows_of(p)], squares_in.at[p], squares_send.at[p],
                      squares_recv.at[p], {"tensor": p})

    def part_copy(p, c):
        return remote(part.at[c, rows_of(p)], part_in.at[t, c], part_send.at[p, c],
                      part_recv.at[t, c], {"tensor": p})

    def part_arrival(p, c):
        return remote(part.at[c, rows_of(p)], part_in.at[p, c], part_send.at[p, c],
                      part_recv.at[p, c], {"tensor": p})

    def hidden_copy(p, c):
        place_at = hidden.at[my_rows, pl.ds(aligned(c * wu, 128), wu)]
        return remote(place_at, place_at, hidden_send.at[p, c], hidden_recv.at[t, c],
                      {"tensor": p})

    def hidden_arrival(p, c):
        place_at = hidden.at[rows_of(p), pl.ds(aligned(c * wu, 128), wu)]
        return remote(place_at, place_at, hidden_send.at[p, c], hidden_recv.at[p, c],
                      {"tensor": p})

    for p in peers:
        squares_copy(p).start()

    @pl.loop(0, nc + LAG)
    def _(c):
        @pl.when(c < nc)
        def _():
            slot = lax.rem(c, nb)
            for copy in gate_copy(c):
                copy.wait()
            part[c, :, :wu] = jnp.dot(
                normed[...], gate_buf[slot], preferred_element_type=f32
            ).astype(bf16)
            part[c, :, wu:] = jnp.dot(
                normed[...], up_buf[slot], preferred_element_type=f32
            ).astype(bf16)
            for p in peers:
                part_copy(p, c).start()

            @pl.when(c + nb < nc)
            def _():
                for copy in gate_copy(c + nb):
                    copy.start()

        @pl.when(c == LAG)
        def _():
            total = squares[my_rows]
            for p in peers:
                squares_arrival(p).wait_recv()
                total = total + squares_in[p]
            mean = jnp.sum(total, axis=1, keepdims=True) / (width * nt)
            squares_in[t] = jnp.broadcast_to(lax.rsqrt(mean + norm_epsilon), (rt, 128))

        @pl.when(c >= LAG)
        def _():
            done = c - LAG
            both = part[done, my_rows].astype(f32)
            for p in peers:
                part_arrival(p, done).wait_recv()
                both = both + part_in[p, done].astype(f32)
            scaling = squares_in[t][:, :1]
            gate = both[:, :wu] * scaling
            up = both[:, wu:] * scaling
            hidden[my_rows, pl.ds(aligned(done * wu, 128), wu)] = (
                gate / (1.0 + jnp.exp(-gate)) * up
            ).astype(bf16)
            for p in peers:
                hidden_copy(p, done).start()

    @pl.loop(0, nc)
    def _(c):
        for p in peers:
            hidden_arrival(p, c).wait_recv()

    pick_slot = lax.broadcasted_iota(jnp.int32, (slots, live), 0)
    pick_row = lax.broadcasted_iota(jnp.int32, (slots, live), 1)
    pick = jnp.where(
        (pick_row == pick_slot + start) & (pick_slot < mine), 1.0, 0.0
    ).astype(bf16)

    def zright_copy(k):
        return remote(zright_out.at[k], zright_in.at[k], zring_send.at[0, k], zring_recv.at[0, k],
                      {"dp": jnp.where(z < n - 1, z + 1, z - 1)})

    def zleft_copy(k):
        return remote(zleft_out.at[k], zleft_in.at[k], zring_send.at[1, k], zring_recv.at[1, k],
                      {"dp": jnp.where(z > 0, z - 1, z + 1)})

    def sib_copy(k):
        return remote(sib_out.at[k], sib_in.at[k], sib_send.at[k], sib_recv.at[k], sib)

    def final_copy(k, side):
        return remote(final_out.at[k], out_buf.at[:, pl.ds(aligned(k * wj + side * hj, 128), hj)],
                      final_send.at[k], final_recv.at[k], sib)

    @pl.loop(0, nj + n)
    def _(m):
        @pl.when(m < nj)
        def _():
            down_copy(m).wait()
            both = jnp.dot(hidden[...], down_buf[m], preferred_element_type=f32)
            low, high = both[:, :hj], both[:, hj:]
            sib_out[m] = jnp.where(s == 0, high, low).astype(bf16)
            sib_copy(m).start()
            partial[m] = jnp.where(s == 0, low, high)

        k = m - 1

        @pl.when((k >= 0) & (k < nj))
        def _():
            sib_copy(k).wait_recv()
            partial[k] = partial[k] + sib_in[k].astype(f32)

        kr, kl, kx = k - z, k - (n - 1 - z), k - far

        @pl.when((kr >= 0) & (kr < nj))
        def _():
            @pl.when(z > 0)
            def _():
                zright_copy(kr).wait_recv()

            @pl.when(z < n - 1)
            def _():
                zright_out[kr] = (partial[kr] + zright_in[kr].astype(f32)).astype(bf16)
                zright_copy(kr).start()

        @pl.when((kl >= 0) & (kl < nj))
        def _():
            @pl.when(z < n - 1)
            def _():
                zleft_copy(kl).wait_recv()

            @pl.when(z > 0)
            def _():
                zleft_out[kl] = (partial[kl] + zleft_in[kl].astype(f32)).astype(bf16)
                zleft_copy(kl).start()

        @pl.when((kx >= 0) & (kx < nj))
        def _():
            total = partial[kx] + zright_in[kx].astype(f32) + zleft_in[kx].astype(f32)
            picked = jnp.dot(pick, total.astype(bf16), preferred_element_type=f32)
            low, high = picked[:hs], picked[hs:]
            final_out[kx] = jnp.where(s == 0, high, low).astype(bf16)
            final_copy(kx, s).start()
            out_buf[:, pl.ds(aligned(kx * wj + s * hj, 128), hj)] = jnp.where(
                s == 0, low, high
            ).astype(bf16)

    @pl.loop(0, nj)
    def _(k):
        final_copy(k, 1 - s).wait_recv()

    out_copy = pltpu.make_async_copy(out_buf, out, out_sem)
    out_copy.start()

    @pl.loop(0, ka)
    def _(k):
        rows_copy(k, s).wait_send()

        @pl.when(z < n - 1)
        def _():
            right_copy(k).wait_send()

        @pl.when(z > 0)
        def _():
            left_copy(k).wait_send()

    for p in peers:
        squares_copy(p).wait_send()

    @pl.loop(0, nc)
    def _(c):
        for p in peers:
            part_copy(p, c).wait_send()
            hidden_copy(p, c).wait_send()

    @pl.loop(0, nj)
    def _(k):
        sib_copy(k).wait_send()
        final_copy(k, s).wait_send()

        @pl.when(z < n - 1)
        def _():
            zright_copy(k).wait_send()

        @pl.when(z > 0)
        def _():
            zleft_copy(k).wait_send()

    out_copy.wait()


def per_device(tokens, norm_gain, gate_weight, up_weight, down_weight, lengths):
    n, nt = lax.axis_size("dp"), lax.axis_size("tensor")
    slots, width = tokens.shape
    units = gate_weight.shape[1]
    live = slots * n * 3 // 8
    rt = live // nt
    ka = 4
    wa = width // 2 // ka
    wu = 256
    nc = units // wu
    nb = min(5, nc)
    wj = 512
    nj = width // wj
    hj, hs = wj // 2, slots // 2
    size = dict(n=n, nt=nt, live=live, slots=slots, ka=ka, wa=wa, nc=nc, wu=wu, nb=nb, nj=nj, wj=wj)
    V, S = pltpu.VMEM, pltpu.SemaphoreType.DMA
    anywhere = pl.BlockSpec(memory_space=pl.ANY)
    return pl.pallas_call(
        functools.partial(kernel, size),
        out_shape=jax.ShapeDtypeStruct((hs, width), bf16),
        in_specs=[
            anywhere,
            pl.BlockSpec(memory_space=pltpu.VMEM),
            anywhere,
            anywhere,
            anywhere,
            pl.BlockSpec(memory_space=pltpu.SMEM),
        ],
        out_specs=anywhere,
        scratch_shapes=[
            V((slots, width), bf16),
            V((nb, width, wu), bf16),
            V((nb, width, wu), bf16),
            V((nj, units, wj), bf16),
            V((ka, live, wa), bf16),
            V((ka, live, wa), bf16),
            V((ka, live, wa), bf16),
            V((ka, live, wa), bf16),
            V((ka, live, wa), bf16),
            V((live, width), bf16),
            V((live, width), bf16),
            V((live, 128), f32),
            V((nt, rt, 128), f32),
            V((nc, live, 2 * wu), bf16),
            V((nt, nc, rt, 2 * wu), bf16),
            V((live, units), bf16),
            V((nj, live, hj), f32),
            V((nj, live, hj), bf16),
            V((nj, live, hj), bf16),
            V((nj, live, hj), bf16),
            V((nj, live, hj), bf16),
            V((nj, live, hj), bf16),
            V((nj, live, hj), bf16),
            V((nj, hs, hj), bf16),
            V((hs, width), bf16),
            S, S((nb,)), S((nb,)), S((nj,)),
            S((2, ka)), S((2, ka)), S((ka,)), S((ka,)), S((nt,)), S((nt,)),
            S((nt, nc)), S((nt, nc)), S((nt, nc)), S((nt, nc)),
            S((nj,)), S((nj,)), S((2, nj)), S((2, nj)), S((nj,)), S((nj,)), S,
        ],
        compiler_params=pltpu.CompilerParams(
            collective_id=0, has_side_effects=True, vmem_limit_bytes=63 * 2**20
        ),
        cost_estimate=pl.CostEstimate(
            flops=6 * live * width * units,
            bytes_accessed=6 * width * units,
            transcendentals=live * units,
        ),
    )(tokens, norm_gain.reshape(1, width), gate_weight, up_weight, down_weight, lengths)


def solution(mesh):
    in_specs = (
        P(("groups", "dp"), "tensor"),
        P("tensor"),
        P("tensor", ("dp", "section")),
        P("tensor", ("dp", "section")),
        P(("dp", "section"), "tensor"),
        P("groups"),
    )
    out_specs = P(("groups", "dp", "section"), "tensor")
    return jax.shard_map(
        per_device, mesh=mesh, in_specs=in_specs, out_specs=out_specs, check_vma=False
    )
```

```python
import functools

import jax
import jax.numpy as jnp
from jax import lax
from jax.experimental import pallas as pl
from jax.experimental.pallas import tpu as pltpu
from jax.sharding import PartitionSpec as P

norm_epsilon = 1e-05
f32, bf16 = jnp.float32, jnp.bfloat16
MESH = pl.DeviceIdType.MESH
LAG = 5
HOP = 3
SIB = 2


def aligned(value, unit):
    return pl.multiple_of(value, unit)


def kernel(
    size,
    tokens, gain, gate_weight, up_weight, down_weight, lengths, out,
    tok, gate_buf, up_buf, down_buf,
    own, right_out, right_in, left_out, left_in, rows, normed, squares, squares_in,
    part, part_in, hidden,
    partial, sib_out, sib_in, zright_out, zright_in, zleft_out, zleft_in, final_out, out_buf,
    tok_sem, gate_sem, up_sem, down_sem,
    ring_send, ring_recv, rows_send, rows_recv, squares_send, squares_recv,
    part_send, part_recv, hidden_send, hidden_recv,
    sib_send, sib_recv, zring_send, zring_recv, final_send, final_recv, out_sem,
):
    n, nt, live, slots = size["n"], size["nt"], size["live"], size["slots"]
    ka, wa, nc, wu, nb, nj, wj = (size[x] for x in ("ka", "wa", "nc", "wu", "nb", "nj", "wj"))
    width = tokens.shape[1]
    half, hj, hs, rt = width // 2, wj // 2, slots // 2, live // nt
    z, t, s = lax.axis_index("dp"), lax.axis_index("tensor"), lax.axis_index("section")
    peers = [lax.rem(t + i, nt) for i in range(1, nt)]
    sib = {"section": 1 - s}
    far = jnp.maximum(z, n - 1 - z)

    def gate_copy(c):
        slot = lax.rem(c, nb)
        cols = pl.ds(aligned(c * wu, 128), wu)
        return (
            pltpu.make_async_copy(gate_weight.at[:, cols], gate_buf.at[slot], gate_sem.at[slot]),
            pltpu.make_async_copy(up_weight.at[:, cols], up_buf.at[slot], up_sem.at[slot]),
        )

    def down_copy(j):
        return pltpu.make_async_copy(
            down_weight.at[:, pl.ds(aligned(j * wj, 128), wj)], down_buf.at[j], down_sem.at[j]
        )

    def remote(src, dst, send, recv, where):
        return pltpu.make_async_remote_copy(
            src_ref=src, dst_ref=dst, send_sem=send, recv_sem=recv, device_id=where,
            device_id_type=MESH,
        )

    tok_copy = pltpu.make_async_copy(tokens, tok, tok_sem)
    tok_copy.start()

    @pl.loop(0, nb)
    def _(c):
        for copy in gate_copy(c):
            copy.start()

    @pl.loop(0, nj)
    def _(j):
        down_copy(j).start()

    barrier = pltpu.get_barrier_semaphore()
    for p in peers:
        pl.semaphore_signal(barrier, inc=1, device_id={"tensor": p}, device_id_type=MESH)
    pl.semaphore_signal(barrier, inc=1, device_id=sib, device_id_type=MESH)

    @pl.when(z > 0)
    def _():
        pl.semaphore_signal(barrier, inc=1, device_id={"dp": z - 1}, device_id_type=MESH)

    @pl.when(z < n - 1)
    def _():
        pl.semaphore_signal(barrier, inc=1, device_id={"dp": z + 1}, device_id_type=MESH)

    start = jnp.int32(0)
    mine = jnp.int32(0)
    for i in range(n):
        start = start + jnp.where(i < z, lengths[i], 0)
        mine = mine + jnp.where(i == z, lengths[i], 0)

    place_row = lax.broadcasted_iota(jnp.int32, (live, slots), 0)
    place_slot = lax.broadcasted_iota(jnp.int32, (live, slots), 1)
    place = jnp.where(
        (place_row == place_slot + start) & (place_slot < mine), 1.0, 0.0
    ).astype(bf16)

    @pl.when(z == 0)
    def _():
        right_in[...] = jnp.zeros_like(right_in)
        zright_in[...] = jnp.zeros_like(zright_in)

    @pl.when(z == n - 1)
    def _():
        left_in[...] = jnp.zeros_like(left_in)
        zleft_in[...] = jnp.zeros_like(zleft_in)

    tok_copy.wait()
    for k in range(ka):
        cols = pl.ds(aligned(s * half + k * wa, 128), wa)
        own[k] = jnp.dot(place, tok[:, cols], preferred_element_type=f32).astype(bf16)

    pl.semaphore_wait(
        barrier, nt + jnp.where(z > 0, 1, 0) + jnp.where(z < n - 1, 1, 0)
    )

    def right_copy(k):
        return remote(right_out.at[k], right_in.at[k], ring_send.at[0, k], ring_recv.at[0, k],
                      {"dp": jnp.where(z < n - 1, z + 1, z - 1)})

    def left_copy(k):
        return remote(left_out.at[k], left_in.at[k], ring_send.at[1, k], ring_recv.at[1, k],
                      {"dp": jnp.where(z > 0, z - 1, z + 1)})

    def rows_copy(k, side):
        cols = pl.ds(aligned(side * half + k * wa, 128), wa)
        return remote(rows.at[:, cols], rows.at[:, cols], rows_send.at[k], rows_recv.at[k], sib)

    squares[...] = jnp.zeros_like(squares)

    def absorb(k, side):
        cols = pl.ds(aligned(side * half + k * wa, 128), wa)
        wide = rows[:, cols].astype(f32)
        total = squares[...]
        for q in range(wa // 128):
            piece = wide[:, q * 128:(q + 1) * 128]
            total = total + piece * piece
        squares[...] = total
        normed[:, cols] = (wide * gain[:, cols]).astype(bf16)

    @pl.loop(0, ka + HOP * (n - 1))
    def _(m):
        kr, kl, kx = m - HOP * z, m - HOP * (n - 1 - z), m - HOP * far

        @pl.when((kr >= 0) & (kr < ka))
        def _():
            @pl.when(z > 0)
            def _():
                right_copy(kr).wait_recv()

            @pl.when(z < n - 1)
            def _():
                right_out[kr] = own[kr] + right_in[kr]
                right_copy(kr).start()

        @pl.when((kl >= 0) & (kl < ka))
        def _():
            @pl.when(z < n - 1)
            def _():
                left_copy(kl).wait_recv()

            @pl.when(z > 0)
            def _():
                left_out[kl] = own[kl] + left_in[kl]
                left_copy(kl).start()

        @pl.when((kx >= 0) & (kx < ka))
        def _():
            cols = pl.ds(aligned(s * half + kx * wa, 128), wa)
            rows[:, cols] = own[kx] + right_in[kx] + left_in[kx]
            rows_copy(kx, s).start()
            absorb(kx, s)

    @pl.loop(0, ka)
    def _(k):
        rows_copy(k, 1 - s).wait_recv()
        absorb(k, 1 - s)

    my_rows = pl.ds(aligned(t * rt, 16), rt)

    def rows_of(p):
        return pl.ds(aligned(p * rt, 16), rt)

    def squares_copy(p):
        return remote(squares.at[rows_of(p)], squares_in.at[t], squares_send.at[p],
                      squares_recv.at[t], {"tensor": p})

    def squares_arrival(p):
        return remote(squares.at[rows_of(p)], squares_in.at[p], squares_send.at[p],
                      squares_recv.at[p], {"tensor": p})

    def part_copy(p, c):
        return remote(part.at[c, rows_of(p)], part_in.at[t, c], part_send.at[p, c],
                      part_recv.at[t, c], {"tensor": p})

    def part_arrival(p, c):
        return remote(part.at[c, rows_of(p)], part_in.at[p, c], part_send.at[p, c],
                      part_recv.at[p, c], {"tensor": p})

    def hidden_copy(p, c):
        place_at = hidden.at[my_rows, pl.ds(aligned(c * wu, 128), wu)]
        return remote(place_at, place_at, hidden_send.at[p, c], hidden_recv.at[t, c],
                      {"tensor": p})

    def hidden_arrival(p, c):
        place_at = hidden.at[rows_of(p), pl.ds(aligned(c * wu, 128), wu)]
        return remote(place_at, place_at, hidden_send.at[p, c], hidden_recv.at[p, c],
                      {"tensor": p})

    for p in peers:
        squares_copy(p).start()

    @pl.loop(0, nc + LAG)
    def _(c):
        @pl.when(c < nc)
        def _():
            slot = lax.rem(c, nb)
            for copy in gate_copy(c):
                copy.wait()
            part[c, :, :wu] = jnp.dot(
                normed[...], gate_buf[slot], preferred_element_type=f32
            ).astype(bf16)
            part[c, :, wu:] = jnp.dot(
                normed[...], up_buf[slot], preferred_element_type=f32
            ).astype(bf16)
            for p in peers:
                part_copy(p, c).start()

            @pl.when(c + nb < nc)
            def _():
                for copy in gate_copy(c + nb):
                    copy.start()

        @pl.when(c == LAG)
        def _():
            total = squares[my_rows]
            for p in peers:
                squares_arrival(p).wait_recv()
                total = total + squares_in[p]
            mean = jnp.sum(total, axis=1, keepdims=True) / (width * nt)
            squares_in[t] = jnp.broadcast_to(lax.rsqrt(mean + norm_epsilon), (rt, 128))

        @pl.when(c >= LAG)
        def _():
            done = c - LAG
            both = part[done, my_rows].astype(f32)
            for p in peers:
                part_arrival(p, done).wait_recv()
                both = both + part_in[p, done].astype(f32)
            scaling = squares_in[t][:, :1]
            gate = both[:, :wu] * scaling
            up = both[:, wu:] * scaling
            hidden[my_rows, pl.ds(aligned(done * wu, 128), wu)] = (
                gate / (1.0 + jnp.exp(-gate)) * up
            ).astype(bf16)
            for p in peers:
                hidden_copy(p, done).start()

    @pl.loop(0, nc)
    def _(c):
        for p in peers:
            hidden_arrival(p, c).wait_recv()

    pick_slot = lax.broadcasted_iota(jnp.int32, (slots, live), 0)
    pick_row = lax.broadcasted_iota(jnp.int32, (slots, live), 1)
    pick = jnp.where(
        (pick_row == pick_slot + start) & (pick_slot < mine), 1.0, 0.0
    ).astype(bf16)

    def zright_copy(k):
        return remote(zright_out.at[k], zright_in.at[k], zring_send.at[0, k], zring_recv.at[0, k],
                      {"dp": jnp.where(z < n - 1, z + 1, z - 1)})

    def zleft_copy(k):
        return remote(zleft_out.at[k], zleft_in.at[k], zring_send.at[1, k], zring_recv.at[1, k],
                      {"dp": jnp.where(z > 0, z - 1, z + 1)})

    def sib_copy(k):
        return remote(sib_out.at[k], sib_in.at[k], sib_send.at[k], sib_recv.at[k], sib)

    def final_copy(k, side):
        return remote(final_out.at[k], out_buf.at[:, pl.ds(aligned(k * wj + side * hj, 128), hj)],
                      final_send.at[k], final_recv.at[k], sib)

    @pl.loop(0, nj + SIB + HOP * (n - 1))
    def _(m):
        @pl.when(m < nj)
        def _():
            down_copy(m).wait()
            both = jnp.dot(hidden[...], down_buf[m], preferred_element_type=f32)
            low, high = both[:, :hj], both[:, hj:]
            sib_out[m] = jnp.where(s == 0, high, low).astype(bf16)
            sib_copy(m).start()
            partial[m] = jnp.where(s == 0, low, high)

        k = m - SIB

        @pl.when((k >= 0) & (k < nj))
        def _():
            sib_copy(k).wait_recv()
            partial[k] = partial[k] + sib_in[k].astype(f32)

        kr, kl, kx = k - HOP * z, k - HOP * (n - 1 - z), k - HOP * far

        @pl.when((kr >= 0) & (kr < nj))
        def _():
            @pl.when(z > 0)
            def _():
                zright_copy(kr).wait_recv()

            @pl.when(z < n - 1)
            def _():
                zright_out[kr] = (partial[kr] + zright_in[kr].astype(f32)).astype(bf16)
                zright_copy(kr).start()

        @pl.when((kl >= 0) & (kl < nj))
        def _():
            @pl.when(z < n - 1)
            def _():
                zleft_copy(kl).wait_recv()

            @pl.when(z > 0)
            def _():
                zleft_out[kl] = (partial[kl] + zleft_in[kl].astype(f32)).astype(bf16)
                zleft_copy(kl).start()

        @pl.when((kx >= 0) & (kx < nj))
        def _():
            total = partial[kx] + zright_in[kx].astype(f32) + zleft_in[kx].astype(f32)
            picked = jnp.dot(pick, total.astype(bf16), preferred_element_type=f32)
            low, high = picked[:hs], picked[hs:]
            final_out[kx] = jnp.where(s == 0, high, low).astype(bf16)
            final_copy(kx, s).start()
            out_buf[:, pl.ds(aligned(kx * wj + s * hj, 128), hj)] = jnp.where(
                s == 0, low, high
            ).astype(bf16)

    @pl.loop(0, nj)
    def _(k):
        final_copy(k, 1 - s).wait_recv()

    out_copy = pltpu.make_async_copy(out_buf, out, out_sem)
    out_copy.start()

    @pl.loop(0, ka)
    def _(k):
        rows_copy(k, s).wait_send()

        @pl.when(z < n - 1)
        def _():
            right_copy(k).wait_send()

        @pl.when(z > 0)
        def _():
            left_copy(k).wait_send()

    for p in peers:
        squares_copy(p).wait_send()

    @pl.loop(0, nc)
    def _(c):
        for p in peers:
            part_copy(p, c).wait_send()
            hidden_copy(p, c).wait_send()

    @pl.loop(0, nj)
    def _(k):
        sib_copy(k).wait_send()
        final_copy(k, s).wait_send()

        @pl.when(z < n - 1)
        def _():
            zright_copy(k).wait_send()

        @pl.when(z > 0)
        def _():
            zleft_copy(k).wait_send()

    out_copy.wait()


def per_device(tokens, norm_gain, gate_weight, up_weight, down_weight, lengths):
    n, nt = lax.axis_size("dp"), lax.axis_size("tensor")
    slots, width = tokens.shape
    units = gate_weight.shape[1]
    live = slots * n * 3 // 8
    rt = live // nt
    ka = min(8, width // 256)
    wa = width // 2 // ka
    wu = 256
    nc = units // wu
    nb = min(5, nc)
    wj = 512
    nj = width // wj
    hj, hs = wj // 2, slots // 2
    size = dict(n=n, nt=nt, live=live, slots=slots, ka=ka, wa=wa, nc=nc, wu=wu, nb=nb, nj=nj, wj=wj)
    V, S = pltpu.VMEM, pltpu.SemaphoreType.DMA
    anywhere = pl.BlockSpec(memory_space=pl.ANY)
    return pl.pallas_call(
        functools.partial(kernel, size),
        out_shape=jax.ShapeDtypeStruct((hs, width), bf16),
        in_specs=[
            anywhere,
            pl.BlockSpec(memory_space=pltpu.VMEM),
            anywhere,
            anywhere,
            anywhere,
            pl.BlockSpec(memory_space=pltpu.SMEM),
        ],
        out_specs=anywhere,
        scratch_shapes=[
            V((slots, width), bf16),
            V((nb, width, wu), bf16),
            V((nb, width, wu), bf16),
            V((nj, units, wj), bf16),
            V((ka, live, wa), bf16),
            V((ka, live, wa), bf16),
            V((ka, live, wa), bf16),
            V((ka, live, wa), bf16),
            V((ka, live, wa), bf16),
            V((live, width), bf16),
            V((live, width), bf16),
            V((live, 128), f32),
            V((nt, rt, 128), f32),
            V((nc, live, 2 * wu), bf16),
            V((nt, nc, rt, 2 * wu), bf16),
            V((live, units), bf16),
            V((nj, live, hj), f32),
            V((nj, live, hj), bf16),
            V((nj, live, hj), bf16),
            V((nj, live, hj), bf16),
            V((nj, live, hj), bf16),
            V((nj, live, hj), bf16),
            V((nj, live, hj), bf16),
            V((nj, hs, hj), bf16),
            V((hs, width), bf16),
            S, S((nb,)), S((nb,)), S((nj,)),
            S((2, ka)), S((2, ka)), S((ka,)), S((ka,)), S((nt,)), S((nt,)),
            S((nt, nc)), S((nt, nc)), S((nt, nc)), S((nt, nc)),
            S((nj,)), S((nj,)), S((2, nj)), S((2, nj)), S((nj,)), S((nj,)), S,
        ],
        compiler_params=pltpu.CompilerParams(
            collective_id=0, has_side_effects=True, vmem_limit_bytes=63 * 2**20
        ),
        cost_estimate=pl.CostEstimate(
            flops=6 * live * width * units,
            bytes_accessed=6 * width * units,
            transcendentals=live * units,
        ),
    )(tokens, norm_gain.reshape(1, width), gate_weight, up_weight, down_weight, lengths)


def solution(mesh):
    in_specs = (
        P(("groups", "dp"), "tensor"),
        P("tensor"),
        P("tensor", ("dp", "section")),
        P("tensor", ("dp", "section")),
        P(("dp", "section"), "tensor"),
        P("groups"),
    )
    out_specs = P(("groups", "dp", "section"), "tensor")
    return jax.shard_map(
        per_device, mesh=mesh, in_specs=in_specs, out_specs=out_specs, check_vma=False
    )
```

```python
import functools

import jax
import jax.numpy as jnp
from jax import lax
from jax.experimental import pallas as pl
from jax.experimental.pallas import tpu as pltpu
from jax.sharding import PartitionSpec as P

norm_epsilon = 1e-05
f32, bf16 = jnp.float32, jnp.bfloat16
MESH = pl.DeviceIdType.MESH
LAG = 8
HOP_ROWS = 4
HOP_SUMS = 3
SIB = 1


def aligned(value, unit):
    return pl.multiple_of(value, unit)


def kernel(
    size,
    tokens, gain_in, gate_weight, up_weight, down_weight, lengths, out,
    tok, gain, gate_buf, up_buf, down_buf,
    own, right_out, right_in, left_out, left_in, rows, normed, squares, squares_in,
    part, part_in, hidden,
    partial, sib_out, sib_in, zright_out, zright_in, zleft_out, zleft_in, final_out, out_buf,
    tok_sem, gain_sem, gate_sem, up_sem, down_sem,
    ring_send, ring_recv, rows_send, rows_recv, squares_send, squares_recv,
    part_send, part_recv, hidden_send, hidden_recv,
    sib_send, sib_recv, zring_send, zring_recv, final_send, final_recv, out_sem,
):
    n, nt, live, slots = size["n"], size["nt"], size["live"], size["slots"]
    ka, wa, nc, wu, nb, nj, wj = (size[x] for x in ("ka", "wa", "nc", "wu", "nb", "nj", "wj"))
    width = tokens.shape[1]
    half, hj, hs, rt = width // 2, wj // 2, slots // 2, live // nt
    z, t, s = lax.axis_index("dp"), lax.axis_index("tensor"), lax.axis_index("section")
    peers = [lax.rem(t + i, nt) for i in range(1, nt)]
    sib = {"section": 1 - s}
    far = jnp.maximum(z, n - 1 - z)

    def gate_copy(c):
        slot = lax.rem(c, nb)
        cols = pl.ds(aligned(c * wu, 128), wu)
        return (
            pltpu.make_async_copy(gate_weight.at[:, cols], gate_buf.at[slot], gate_sem.at[slot]),
            pltpu.make_async_copy(up_weight.at[:, cols], up_buf.at[slot], up_sem.at[slot]),
        )

    def down_copy(j):
        return pltpu.make_async_copy(
            down_weight.at[:, pl.ds(aligned(j * wj, 128), wj)], down_buf.at[j], down_sem.at[j]
        )

    def remote(src, dst, send, recv, where):
        return pltpu.make_async_remote_copy(
            src_ref=src, dst_ref=dst, send_sem=send, recv_sem=recv, device_id=where,
            device_id_type=MESH,
        )

    tok_copy = pltpu.make_async_copy(tokens, tok, tok_sem)
    tok_copy.start()
    gain_copy = pltpu.make_async_copy(gain_in, gain, gain_sem)
    gain_copy.start()

    @pl.loop(0, nb)
    def _(c):
        for copy in gate_copy(c):
            copy.start()

    @pl.loop(0, nj)
    def _(j):
        down_copy(j).start()

    barrier = pltpu.get_barrier_semaphore()
    for p in peers:
        pl.semaphore_signal(barrier, inc=1, device_id={"tensor": p}, device_id_type=MESH)
    pl.semaphore_signal(barrier, inc=1, device_id=sib, device_id_type=MESH)

    @pl.when(z > 0)
    def _():
        pl.semaphore_signal(barrier, inc=1, device_id={"dp": z - 1}, device_id_type=MESH)

    @pl.when(z < n - 1)
    def _():
        pl.semaphore_signal(barrier, inc=1, device_id={"dp": z + 1}, device_id_type=MESH)

    start = jnp.int32(0)
    mine = jnp.int32(0)
    for i in range(n):
        start = start + jnp.where(i < z, lengths[i], 0)
        mine = mine + jnp.where(i == z, lengths[i], 0)

    place_row = lax.broadcasted_iota(jnp.int32, (live, slots), 0)
    place_slot = lax.broadcasted_iota(jnp.int32, (live, slots), 1)
    place = jnp.where(
        (place_row == place_slot + start) & (place_slot < mine), 1.0, 0.0
    ).astype(bf16)

    @pl.when(z == 0)
    def _():
        right_in[...] = jnp.zeros_like(right_in)
        zright_in[...] = jnp.zeros_like(zright_in)

    @pl.when(z == n - 1)
    def _():
        left_in[...] = jnp.zeros_like(left_in)
        zleft_in[...] = jnp.zeros_like(zleft_in)

    tok_copy.wait()
    gain_copy.wait()
    for k in range(ka):
        cols = pl.ds(aligned(s * half + k * wa, 128), wa)
        own[k] = jnp.dot(place, tok[:, cols], preferred_element_type=f32).astype(bf16)

    pl.semaphore_wait(
        barrier, nt + jnp.where(z > 0, 1, 0) + jnp.where(z < n - 1, 1, 0)
    )

    def right_copy(k):
        return remote(right_out.at[k], right_in.at[k], ring_send.at[0, k], ring_recv.at[0, k],
                      {"dp": jnp.where(z < n - 1, z + 1, z - 1)})

    def left_copy(k):
        return remote(left_out.at[k], left_in.at[k], ring_send.at[1, k], ring_recv.at[1, k],
                      {"dp": jnp.where(z > 0, z - 1, z + 1)})

    def rows_copy(k, side):
        cols = pl.ds(aligned(side * half + k * wa, 128), wa)
        return remote(rows.at[:, cols], rows.at[:, cols], rows_send.at[k], rows_recv.at[k], sib)

    squares[...] = jnp.zeros_like(squares)

    def absorb(k, side):
        cols = pl.ds(aligned(side * half + k * wa, 128), wa)
        wide = rows[:, cols].astype(f32)
        total = squares[...]
        for q in range(wa // 128):
            piece = wide[:, q * 128:(q + 1) * 128]
            total = total + piece * piece
        squares[...] = total
        normed[:, cols] = (wide * gain[:, cols]).astype(bf16)

    @pl.loop(0, ka + HOP_ROWS * (n - 1))
    def _(m):
        kr, kl, kx = m - HOP_ROWS * z, m - HOP_ROWS * (n - 1 - z), m - HOP_ROWS * far

        @pl.when((kr >= 0) & (kr < ka))
        def _():
            @pl.when(z > 0)
            def _():
                right_copy(kr).wait_recv()

            @pl.when(z < n - 1)
            def _():
                right_out[kr] = own[kr] + right_in[kr]
                right_copy(kr).start()

        @pl.when((kl >= 0) & (kl < ka))
        def _():
            @pl.when(z < n - 1)
            def _():
                left_copy(kl).wait_recv()

            @pl.when(z > 0)
            def _():
                left_out[kl] = own[kl] + left_in[kl]
                left_copy(kl).start()

        @pl.when((kx >= 0) & (kx < ka))
        def _():
            cols = pl.ds(aligned(s * half + kx * wa, 128), wa)
            rows[:, cols] = own[kx] + right_in[kx] + left_in[kx]
            rows_copy(kx, s).start()
            absorb(kx, s)

    @pl.loop(0, ka)
    def _(k):
        rows_copy(k, 1 - s).wait_recv()
        absorb(k, 1 - s)

    my_rows = pl.ds(aligned(t * rt, 16), rt)

    def rows_of(p):
        return pl.ds(aligned(p * rt, 16), rt)

    def squares_copy(p):
        return remote(squares.at[rows_of(p)], squares_in.at[t], squares_send.at[p],
                      squares_recv.at[t], {"tensor": p})

    def squares_arrival(p):
        return remote(squares.at[rows_of(p)], squares_in.at[p], squares_send.at[p],
                      squares_recv.at[p], {"tensor": p})

    def part_copy(p, c):
        return remote(part.at[c, rows_of(p)], part_in.at[t, c], part_send.at[p, c],
                      part_recv.at[t, c], {"tensor": p})

    def part_arrival(p, c):
        return remote(part.at[c, rows_of(p)], part_in.at[p, c], part_send.at[p, c],
                      part_recv.at[p, c], {"tensor": p})

    def hidden_copy(p, c):
        place_at = hidden.at[my_rows, pl.ds(aligned(c * wu, 128), wu)]
        return remote(place_at, place_at, hidden_send.at[p, c], hidden_recv.at[t, c],
                      {"tensor": p})

    def hidden_arrival(p, c):
        place_at = hidden.at[rows_of(p), pl.ds(aligned(c * wu, 128), wu)]
        return remote(place_at, place_at, hidden_send.at[p, c], hidden_recv.at[p, c],
                      {"tensor": p})

    for p in peers:
        squares_copy(p).start()

    @pl.loop(0, nc + LAG)
    def _(c):
        @pl.when(c < nc)
        def _():
            slot = lax.rem(c, nb)
            for copy in gate_copy(c):
                copy.wait()
            part[c, :, :wu] = jnp.dot(
                normed[...], gate_buf[slot], preferred_element_type=f32
            ).astype(bf16)
            part[c, :, wu:] = jnp.dot(
                normed[...], up_buf[slot], preferred_element_type=f32
            ).astype(bf16)
            for p in peers:
                part_copy(p, c).start()

            @pl.when(c + nb < nc)
            def _():
                for copy in gate_copy(c + nb):
                    copy.start()

        @pl.when(c == LAG)
        def _():
            total = squares[my_rows]
            for p in peers:
                squares_arrival(p).wait_recv()
                total = total + squares_in[p]
            mean = jnp.sum(total, axis=1, keepdims=True) / (width * nt)
            squares_in[t] = jnp.broadcast_to(lax.rsqrt(mean + norm_epsilon), (rt, 128))

        @pl.when(c >= LAG)
        def _():
            done = c - LAG
            both = part[done, my_rows].astype(f32)
            for p in peers:
                part_arrival(p, done).wait_recv()
                both = both + part_in[p, done].astype(f32)
            scaling = squares_in[t][:, :1]
            gate = both[:, :wu] * scaling
            up = both[:, wu:] * scaling
            hidden[my_rows, pl.ds(aligned(done * wu, 128), wu)] = (
                gate / (1.0 + jnp.exp(-gate)) * up
            ).astype(bf16)
            for p in peers:
                hidden_copy(p, done).start()

    @pl.loop(0, nc)
    def _(c):
        for p in peers:
            hidden_arrival(p, c).wait_recv()

    pick_slot = lax.broadcasted_iota(jnp.int32, (slots, live), 0)
    pick_row = lax.broadcasted_iota(jnp.int32, (slots, live), 1)
    pick = jnp.where(
        (pick_row == pick_slot + start) & (pick_slot < mine), 1.0, 0.0
    ).astype(bf16)

    def zright_copy(k):
        return remote(zright_out.at[k], zright_in.at[k], zring_send.at[0, k], zring_recv.at[0, k],
                      {"dp": jnp.where(z < n - 1, z + 1, z - 1)})

    def zleft_copy(k):
        return remote(zleft_out.at[k], zleft_in.at[k], zring_send.at[1, k], zring_recv.at[1, k],
                      {"dp": jnp.where(z > 0, z - 1, z + 1)})

    def sib_copy(k):
        return remote(sib_out.at[k], sib_in.at[k], sib_send.at[k], sib_recv.at[k], sib)

    def final_copy(k, side):
        return remote(final_out.at[k], out_buf.at[:, pl.ds(aligned(k * wj + side * hj, 128), hj)],
                      final_send.at[k], final_recv.at[k], sib)

    @pl.loop(0, nj + SIB + HOP_SUMS * (n - 1))
    def _(m):
        @pl.when(m < nj)
        def _():
            down_copy(m).wait()
            both = jnp.dot(hidden[...], down_buf[m], preferred_element_type=f32)
            low, high = both[:, :hj], both[:, hj:]
            sib_out[m] = jnp.where(s == 0, high, low).astype(bf16)
            sib_copy(m).start()
            partial[m] = jnp.where(s == 0, low, high)

        k = m - SIB

        @pl.when((k >= 0) & (k < nj))
        def _():
            sib_copy(k).wait_recv()
            partial[k] = partial[k] + sib_in[k].astype(f32)

        kr, kl, kx = k - HOP_SUMS * z, k - HOP_SUMS * (n - 1 - z), k - HOP_SUMS * far

        @pl.when((kr >= 0) & (kr < nj))
        def _():
            @pl.when(z > 0)
            def _():
                zright_copy(kr).wait_recv()

            @pl.when(z < n - 1)
            def _():
                zright_out[kr] = (partial[kr] + zright_in[kr].astype(f32)).astype(bf16)
                zright_copy(kr).start()

        @pl.when((kl >= 0) & (kl < nj))
        def _():
            @pl.when(z < n - 1)
            def _():
                zleft_copy(kl).wait_recv()

            @pl.when(z > 0)
            def _():
                zleft_out[kl] = (partial[kl] + zleft_in[kl].astype(f32)).astype(bf16)
                zleft_copy(kl).start()

        @pl.when((kx >= 0) & (kx < nj))
        def _():
            total = partial[kx] + zright_in[kx].astype(f32) + zleft_in[kx].astype(f32)
            picked = jnp.dot(pick, total.astype(bf16), preferred_element_type=f32)
            low, high = picked[:hs], picked[hs:]
            final_out[kx] = jnp.where(s == 0, high, low).astype(bf16)
            final_copy(kx, s).start()
            out_buf[:, pl.ds(aligned(kx * wj + s * hj, 128), hj)] = jnp.where(
                s == 0, low, high
            ).astype(bf16)

    @pl.loop(0, nj)
    def _(k):
        final_copy(k, 1 - s).wait_recv()

    out_copy = pltpu.make_async_copy(out_buf, out, out_sem)
    out_copy.start()

    @pl.loop(0, ka)
    def _(k):
        rows_copy(k, s).wait_send()

        @pl.when(z < n - 1)
        def _():
            right_copy(k).wait_send()

        @pl.when(z > 0)
        def _():
            left_copy(k).wait_send()

    for p in peers:
        squares_copy(p).wait_send()

    @pl.loop(0, nc)
    def _(c):
        for p in peers:
            part_copy(p, c).wait_send()
            hidden_copy(p, c).wait_send()

    @pl.loop(0, nj)
    def _(k):
        sib_copy(k).wait_send()
        final_copy(k, s).wait_send()

        @pl.when(z < n - 1)
        def _():
            zright_copy(k).wait_send()

        @pl.when(z > 0)
        def _():
            zleft_copy(k).wait_send()

    out_copy.wait()


def per_device(tokens, norm_gain, gate_weight, up_weight, down_weight, lengths):
    n, nt = lax.axis_size("dp"), lax.axis_size("tensor")
    slots, width = tokens.shape
    units = gate_weight.shape[1]
    live = slots * n * 3 // 8
    rt = live // nt
    ka = min(8, width // 256)
    wa = width // 2 // ka
    wu = 256
    nc = units // wu
    nb = min(5, nc)
    wj = 512
    nj = width // wj
    hj, hs = wj // 2, slots // 2
    size = dict(n=n, nt=nt, live=live, slots=slots, ka=ka, wa=wa, nc=nc, wu=wu, nb=nb, nj=nj, wj=wj)
    V, S = pltpu.VMEM, pltpu.SemaphoreType.DMA
    anywhere = pl.BlockSpec(memory_space=pl.ANY)
    return pl.pallas_call(
        functools.partial(kernel, size),
        out_shape=jax.ShapeDtypeStruct((hs, width), bf16),
        in_specs=[
            anywhere,
            anywhere,
            anywhere,
            anywhere,
            anywhere,
            pl.BlockSpec(memory_space=pltpu.SMEM),
        ],
        out_specs=anywhere,
        scratch_shapes=[
            V((slots, width), bf16),
            V((1, width), f32),
            V((nb, width, wu), bf16),
            V((nb, width, wu), bf16),
            V((nj, units, wj), bf16),
            V((ka, live, wa), bf16),
            V((ka, live, wa), bf16),
            V((ka, live, wa), bf16),
            V((ka, live, wa), bf16),
            V((ka, live, wa), bf16),
            V((live, width), bf16),
            V((live, width), bf16),
            V((live, 128), f32),
            V((nt, rt, 128), f32),
            V((nc, live, 2 * wu), bf16),
            V((nt, nc, rt, 2 * wu), bf16),
            V((live, units), bf16),
            V((nj, live, hj), f32),
            V((nj, live, hj), bf16),
            V((nj, live, hj), bf16),
            V((nj, live, hj), bf16),
            V((nj, live, hj), bf16),
            V((nj, live, hj), bf16),
            V((nj, live, hj), bf16),
            V((nj, hs, hj), bf16),
            V((hs, width), bf16),
            S, S, S((nb,)), S((nb,)), S((nj,)),
            S((2, ka)), S((2, ka)), S((ka,)), S((ka,)), S((nt,)), S((nt,)),
            S((nt, nc)), S((nt, nc)), S((nt, nc)), S((nt, nc)),
            S((nj,)), S((nj,)), S((2, nj)), S((2, nj)), S((nj,)), S((nj,)), S,
        ],
        compiler_params=pltpu.CompilerParams(
            collective_id=0, has_side_effects=True, vmem_limit_bytes=63 * 2**20
        ),
        cost_estimate=pl.CostEstimate(
            flops=6 * live * width * units,
            bytes_accessed=6 * width * units,
            transcendentals=live * units,
        ),
    )(tokens, norm_gain.reshape(1, width), gate_weight, up_weight, down_weight, lengths)


def solution(mesh):
    in_specs = (
        P(("groups", "dp"), "tensor"),
        P("tensor"),
        P("tensor", ("dp", "section")),
        P("tensor", ("dp", "section")),
        P(("dp", "section"), "tensor"),
        P("groups"),
    )
    out_specs = P(("groups", "dp", "section"), "tensor")
    return jax.shard_map(
        per_device, mesh=mesh, in_specs=in_specs, out_specs=out_specs, check_vma=False
    )
```
